32 devices in a mesh: ctx: 8 (over y, x, core), feat: 4 (over z).
Axes of the slice: x: 2, y: 2, z: 4, core: 2. Of those that a mesh axis runs over, the one named last changes fastest.
Arguments:
- tokens: bfloat16 [4, 2048, 8192], P(None, 'ctx', 'feat'), may hold values from -128 to 128
- norm_gain: float32 [8192], P('feat'), may hold values from 0.1 to 1.9
- qkv_weight: bfloat16 [3, 32, 6, 256, 256], P(None, 'feat'), may hold values from -1 to 1
- out_weight: bfloat16 [32, 6, 256, 256], P('feat'), may hold values from -0.15625 to 0.15625
- section_bits: int32 [5], replicated, may hold values from 0 to 4, each once
- positions: int32 [4, 2048], P(None, 'ctx'), may hold values from 0 to 128, as said below
Outputs:
- layer_out: float32 [4, 2048, 8192], P(None, 'ctx', 'feat')
The draws below stay inside these ranges and needn't reach their ends.
Inputs may be any that keep to these rules, and one draw needn't show every extreme that they name: Within a document, positions rise by one from token to token until they reach 128, where they stay; a document starts at position 0, except the first of a sequence, which may start above 0.
All inputs are finite; a program needn't handle non-finite values.
Results may differ from the reference program's by a relative error of at most 0.0064.
Values may be sent and summed in bfloat16 or wider, within the bound.
A program may use at most 256 MiB of HBM per device.

```python
import jax
import jax.numpy as jnp
from jax import lax

D = 8192
HEADS = 64
BLOCK = 256
SECTIONS = 5
WINDOW = 128
SEQS = 4
TOK_DEV = 256
NB = 32
HEAD = 128
SEQ_LEN = 2048


def draw_tokens(key, part):
    key_col, key_base = jax.random.split(jax.random.fold_in(key, 11), 2)
    column = jnp.exp(jax.random.uniform(key_col, (D,), jnp.float32, -0.7, 0.7))
    column = column * 3.0 ** (jnp.arange(D, dtype=jnp.float32) / D)
    values = jax.random.truncated_normal(key_base, -4.0, 4.0, (SEQS, SEQ_LEN, D), jnp.float32) * column
    return values.astype(jnp.bfloat16)


def draw_qkv_weight(key, part):
    fan = (SECTIONS + 1) * BLOCK
    shape = (3, NB, SECTIONS + 1, BLOCK, BLOCK)
    values = jax.random.truncated_normal(jax.random.fold_in(key, 23), -4.0, 4.0, shape, jnp.float32) * fan ** (-0.5)
    values = jnp.clip(values, -1.0, 1.0)
    return values.astype(jnp.bfloat16)


def draw_positions(key, part):
    key_start, key_offset = jax.random.split(jax.random.fold_in(key, 37))
    index = jnp.arange(SEQ_LEN, dtype=jnp.int32)
    starts = jax.random.randint(key_start, (SEQS, SEQ_LEN), 0, 3 * TOK_DEV) == 0
    starts = starts & (index > WINDOW)[None, :]
    starts = starts | (index == 0)[None, :]
    latest = lax.cummax(jnp.where(starts, index[None, :], 0), axis=1)
    offset = jax.random.randint(key_offset, (SEQS, 1), 0, 2 * WINDOW)
    raw = index[None, :] - latest + jnp.where(latest == 0, offset, 0)
    return jnp.minimum(raw, WINDOW).astype(jnp.int32)


def level_of(key, extent, pieces, smallest, top_value):
    level = 1.0
    for axis_at, shards_of in pieces:
        draws = jax.random.uniform(jax.random.fold_in(jax.random.fold_in(key, 6), axis_at), (shards_of,), jnp.float32, smallest / len(pieces), top_value / len(pieces))
        level = level * jnp.repeat(jnp.exp(draws), extent[axis_at] // shards_of).reshape((-1,) + (1,) * (len(extent) - 1 - axis_at))
    return level


def centred(key, shape, scale, limit, pieces=(), kind=jnp.bfloat16):
    values = jax.random.normal(key, shape, jnp.float32) * scale
    if len(pieces) > 0:
        values = level_of(key, shape, pieces, -0.22, 0.18) * values
    return jnp.clip(values, min=-limit, max=limit).astype(kind)


def setup_inputs(seed: int = 0) -> dict:
    seeds = jax.random.split(jax.random.key(seed), 7)
    return {
        "tokens": draw_tokens(jax.random.fold_in(seeds[6], 71), 0),
        "norm_gain": jnp.clip(1.0 + 0.18 * jax.random.normal(seeds[1], (D,), jnp.float32), 0.1, 1.9),
        "qkv_weight": draw_qkv_weight(jax.random.fold_in(seeds[6], 71), 0),
        "out_weight": centred(seeds[3], (NB, SECTIONS + 1, BLOCK, BLOCK), ((SECTIONS + 1) * BLOCK) ** -0.5, 0.15625, ((0, 4),)),
        "section_bits": jax.random.permutation(seeds[4], SECTIONS).astype(jnp.int32),
        "positions": draw_positions(jax.random.fold_in(seeds[6], 71), 0),
    }


def apply_butterfly(blocks, weight, section_bits):
    index = jnp.arange(NB, dtype=jnp.int32)
    total = jnp.einsum('rnk,nkj->rnj', blocks.astype(jnp.float32), weight[:, 0].astype(jnp.float32))
    for section in range(1, SECTIONS + 1):
        flip = jnp.left_shift(jnp.int32(1), section_bits[section - 1].astype(jnp.int32))
        partner = jnp.bitwise_xor(index, flip).astype(jnp.int32)
        moved = jnp.take(blocks, partner, axis=1)
        total = total + jnp.einsum('rnk,nkj->rnj', moved.astype(jnp.float32), weight[:, section].astype(jnp.float32))
    return total

def reference(tokens, norm_gain, qkv_weight, out_weight, section_bits, positions):
    seqs, length, width = tokens.shape
    x_full = tokens.astype(jnp.float32)
    mean_sq = lax.optimization_barrier(jnp.mean(x_full * x_full, axis=-1, keepdims=True))
    normed = (x_full * lax.rsqrt(mean_sq + 1e-05) * norm_gain).astype(jnp.bfloat16)
    blocks = normed.reshape(seqs * length, NB, BLOCK)
    projected = []
    for matrix in range(3):
        part = apply_butterfly(blocks, qkv_weight[matrix], section_bits).astype(jnp.bfloat16)
        projected.append(part.reshape(seqs, length, HEADS, HEAD))
    query, keys, values = projected
    keys_pad = jnp.pad(keys, ((0, 0), (WINDOW, 0), (0, 0), (0, 0)))
    values_pad = jnp.pad(values, ((0, 0), (WINDOW, 0), (0, 0), (0, 0)))
    scale = HEAD ** (-0.5)

    def one_block(cidx):
        start = cidx * WINDOW
        qblock = lax.dynamic_slice_in_dim(query, start, WINDOW, 1)
        kblock = lax.dynamic_slice_in_dim(keys_pad, start, 2 * WINDOW, 1)
        vblock = lax.dynamic_slice_in_dim(values_pad, start, 2 * WINDOW, 1)
        pblock = lax.dynamic_slice_in_dim(positions, start, WINDOW, 1)
        scores = jnp.einsum('sqhd,skhd->shqk', qblock.astype(jnp.float32), kblock.astype(jnp.float32)) * scale
        qpos = jnp.arange(WINDOW, dtype=jnp.int32)
        kpos = jnp.arange(2 * WINDOW, dtype=jnp.int32)
        dist = qpos[:, None] + WINDOW - kpos[None, :]
        key_index = start + kpos - WINDOW
        valid = (dist >= 0) & (dist < WINDOW) & (key_index >= 0)[None, :]
        valid = valid[None] & (dist[None] <= pblock[:, :, None])
        masked = jnp.where(valid[:, None], scores, -1e+30)
        top = lax.optimization_barrier(jnp.max(masked, axis=-1, keepdims=True))
        expo = jnp.exp(masked - top)
        weights = (expo / lax.optimization_barrier(jnp.sum(expo, axis=-1, keepdims=True))).astype(jnp.bfloat16)
        mixed = jnp.einsum('shqk,skhd->sqhd', weights.astype(jnp.float32), vblock.astype(jnp.float32))
        return mixed.astype(jnp.bfloat16)
    attended = lax.map(one_block, jnp.arange(length // WINDOW, dtype=jnp.int32))
    attended = jnp.transpose(attended, (1, 0, 2, 3, 4)).reshape(seqs * length, NB, BLOCK)
    projected_out = apply_butterfly(attended, out_weight, section_bits).reshape(seqs, length, width)
    return x_full + projected_out
```

```python
import functools

import jax
import jax.numpy as jnp
from jax import lax
from jax.experimental import pallas as pl
from jax.experimental.pallas import tpu as pltpu
from jax.sharding import PartitionSpec as P

D = 8192
WINDOW = 128
HEAD = 128
VMEM_LIMIT = 48 * 2**20


def swapped(value, axis, bit):
    mask = 2**bit
    pairs = [(source, source ^ mask) for source in range(lax.axis_size(axis))]
    return lax.ppermute(value, axis, pairs)


def passed_along(shard, axis, by):
    devices = lax.axis_size(axis)
    pairs = [(i, i + by) for i in range(devices) if 0 <= i + by < devices]
    return lax.ppermute(shard, axis, pairs)


def params():
    return pltpu.CompilerParams(
        dimension_semantics=("arbitrary",), vmem_limit_bytes=VMEM_LIMIT
    )


def partner_slots(bits_ref, i, local_blocks, sections):
    local_bits = local_blocks.bit_length() - 1
    slots = [i]
    for s in range(sections):
        bit = bits_ref[s]
        near = lax.bitwise_xor(i, lax.shift_left(jnp.int32(1), bit))
        far = (1 + bit - local_bits) * local_blocks + i
        slots.append(jnp.where(bit < local_bits, near, far))
    return slots


def stage_kernel(x_ref, *rest):
    rest[-1][...] = x_ref[0]


def stage(tokens, s, after):
    seqs, rows, width = tokens.shape
    return pl.pallas_call(
        stage_kernel,
        grid=(1,),
        in_specs=[pl.BlockSpec((1, rows, width), lambda i: (s, 0, 0))]
        + [pl.BlockSpec(memory_space=pl.ANY)] * len(after),
        out_specs=pl.BlockSpec((rows, width), lambda i: (0, 0)),
        out_shape=jax.ShapeDtypeStruct((rows, width), tokens.dtype),
        compiler_params=params(),
        cost_estimate=pl.CostEstimate(
            flops=0, bytes_accessed=4 * rows * width, transcendentals=0
        ),
        name="stage",
    )(tokens, *after)


def qkv_kernel(parts, local_blocks, sections, bits_ref, *refs):
    x_refs = refs[:parts]
    scale_ref, gain_ref, w_ref, q_ref, kv_ref, tail_ref, normed = refs[parts:]
    i = pl.program_id(0)
    block = w_ref.shape[-1]

    @pl.when(i == 0)
    def _():
        scale = scale_ref[0]
        for part in range(parts):
            for b in range(local_blocks):
                lanes = slice(b * block, (b + 1) * block)
                x = x_refs[part][0, :, lanes] if part == 0 else x_refs[part][:, lanes]
                x = x.astype(jnp.float32) * scale * gain_ref[part : part + 1, lanes]
                normed[part * local_blocks + b] = x.astype(jnp.bfloat16)

    slots = partner_slots(bits_ref, i, local_blocks, sections)
    lhs = jnp.concatenate([normed[slot] for slot in slots], axis=1)
    rows = lhs.shape[0]
    for m in range(3):
        out = jnp.dot(lhs, w_ref[m, 0], preferred_element_type=jnp.float32)
        out = out.astype(jnp.bfloat16)
        if m == 0:
            q_ref[...] = out
        else:
            kv_ref[m - 1] = out
            tail_ref[m - 1] = out[rows - WINDOW :]


def project(section_bits, tokens, s, partners, scale, gains, weight):
    seqs, rows, width = tokens.shape
    _, local_blocks, depth, block = weight.shape
    sections = section_bits.shape[0]
    parts = 1 + len(partners)
    whole = lambda i, bits: (0, 0)
    bf16 = jnp.bfloat16
    return pl.pallas_call(
        functools.partial(qkv_kernel, parts, local_blocks, sections),
        grid_spec=pltpu.PrefetchScalarGridSpec(
            num_scalar_prefetch=1,
            grid=(local_blocks,),
            in_specs=[pl.BlockSpec((1, rows, width), lambda i, bits: (s, 0, 0))]
            + [pl.BlockSpec((rows, width), whole)] * len(partners)
            + [
                pl.BlockSpec((1, rows, 1), lambda i, bits: (s, 0, 0)),
                pl.BlockSpec((parts, width), whole),
                pl.BlockSpec((3, 1, depth, block), lambda i, bits: (0, i, 0, 0)),
            ],
            out_specs=[
                pl.BlockSpec((rows, block), lambda i, bits: (0, i)),
                pl.BlockSpec((2, rows, block), lambda i, bits: (0, 0, i)),
                pl.BlockSpec((2, WINDOW, block), lambda i, bits: (0, 0, i)),
            ],
            scratch_shapes=[pltpu.VMEM((parts * local_blocks, rows, block), bf16)],
        ),
        out_shape=[
            jax.ShapeDtypeStruct((rows, width), bf16),
            jax.ShapeDtypeStruct((2, rows, width), bf16),
            jax.ShapeDtypeStruct((2, WINDOW, width), bf16),
        ],
        compiler_params=params(),
        cost_estimate=pl.CostEstimate(
            flops=6 * rows * depth * width,
            bytes_accessed=2 * weight.size + 2 * rows * width * (parts + 4),
            transcendentals=0,
        ),
        name="project",
    )(section_bits, tokens, *partners, scale, gains, weight)


def attend_kernel(q_ref, kv_ref, rim_ref, reach_ref, out_ref):
    rows, width = q_ref.shape
    for c in range(rows // WINDOW):
        here = slice(c * WINDOW, (c + 1) * WINDOW)
        row = lax.broadcasted_iota(jnp.int32, (WINDOW, 2 * WINDOW), 0)
        col = lax.broadcasted_iota(jnp.int32, (WINDOW, 2 * WINDOW), 1)
        dist = row + WINDOW - col
        valid = (dist >= 0) & (dist <= reach_ref[0, here])
        for h in range(width // HEAD):
            lanes = slice(h * HEAD, (h + 1) * HEAD)
            near = []
            for m in range(2):
                if c == 0:
                    before = rim_ref[m, :, lanes]
                else:
                    before = kv_ref[m, (c - 1) * WINDOW : c * WINDOW, lanes]
                near.append(jnp.concatenate([before, kv_ref[m, here, lanes]], axis=0))
            scores = lax.dot_general(
                q_ref[here, lanes],
                near[0],
                (((1,), (1,)), ((), ())),
                preferred_element_type=jnp.float32,
            )
            masked = jnp.where(valid, scores * HEAD ** (-0.5), -1e30)
            top = jnp.max(masked, axis=-1, keepdims=True)
            expo = jnp.exp(masked - top)
            total = jnp.sum(expo, axis=-1, keepdims=True)
            weights = (expo * (1.0 / total)).astype(jnp.bfloat16)
            mixed = jnp.dot(weights, near[1], preferred_element_type=jnp.float32)
            out_ref[here, lanes] = mixed.astype(jnp.bfloat16)


def attend(q, kv, rim, reach, s):
    rows, width = q.shape
    step = min(width, 4 * HEAD)
    return pl.pallas_call(
        attend_kernel,
        grid=(width // step,),
        in_specs=[
            pl.BlockSpec((rows, step), lambda i: (0, i)),
            pl.BlockSpec((2, rows, step), lambda i: (0, 0, i)),
            pl.BlockSpec((2, WINDOW, step), lambda i: (0, 0, i)),
            pl.BlockSpec((1, rows, 1), lambda i: (s, 0, 0)),
        ],
        out_specs=pl.BlockSpec((rows, step), lambda i: (0, i)),
        out_shape=jax.ShapeDtypeStruct((rows, width), jnp.bfloat16),
        compiler_params=params(),
        cost_estimate=pl.CostEstimate(
            flops=8 * rows * WINDOW * width,
            bytes_accessed=2 * rows * width * 5,
            transcendentals=2 * rows * WINDOW * (width // HEAD),
        ),
        name="attend",
    )(q, kv, rim, reach)


def out_kernel(parts, local_blocks, sections, bits_ref, *refs):
    a_refs = refs[:parts]
    x_ref, w_ref = refs[parts : parts + 2]
    out_ref, gathered = refs[-2:]
    i = pl.program_id(0)
    block = w_ref.shape[-1]

    @pl.when(i == 0)
    def _():
        for part in range(parts):
            for b in range(local_blocks):
                lanes = slice(b * block, (b + 1) * block)
                gathered[part * local_blocks + b] = a_refs[part][:, lanes]

    slots = partner_slots(bits_ref, i, local_blocks, sections)
    lhs = jnp.concatenate([gathered[slot] for slot in slots], axis=1)
    out = jnp.dot(lhs, w_ref[0], preferred_element_type=jnp.float32)
    out_ref[0] = x_ref[0].astype(jnp.float32) + out


def finish(section_bits, blocks, tokens, s, weight, result):
    seqs, rows, width = tokens.shape
    local_blocks, depth, block = weight.shape
    sections = section_bits.shape[0]
    parts = len(blocks)
    one = lambda i, bits: (s, 0, i)
    earlier = [] if result is None else [result]
    return pl.pallas_call(
        functools.partial(out_kernel, parts, local_blocks, sections),
        grid_spec=pltpu.PrefetchScalarGridSpec(
            num_scalar_prefetch=1,
            grid=(local_blocks,),
            in_specs=[pl.BlockSpec((rows, width), lambda i, bits: (0, 0))] * parts
            + [
                pl.BlockSpec((1, rows, block), one),
                pl.BlockSpec((1, depth, block), lambda i, bits: (i, 0, 0)),
            ]
            + [pl.BlockSpec(memory_space=pl.ANY)] * len(earlier),
            out_specs=pl.BlockSpec((1, rows, block), one),
            scratch_shapes=[
                pltpu.VMEM((parts * local_blocks, rows, block), jnp.bfloat16)
            ],
        ),
        out_shape=jax.ShapeDtypeStruct(tokens.shape, jnp.float32),
        input_output_aliases={} if result is None else {3 + parts: 0},
        compiler_params=params(),
        cost_estimate=pl.CostEstimate(
            flops=2 * rows * depth * width,
            bytes_accessed=2 * weight.size + rows * width * (2 * parts + 6),
            transcendentals=0,
        ),
        name="finish",
    )(section_bits, *blocks, tokens, weight, *earlier)


def per_device(tokens, norm_gain, qkv_weight, out_weight, section_bits, positions):
    seqs, rows, width = tokens.shape
    _, local_blocks, terms, block, _ = qkv_weight.shape
    device_bits = lax.axis_size("feat").bit_length() - 1
    far_first = list(range(device_bits))[::-1]
    qkv_weight = qkv_weight.reshape(3, local_blocks, terms * block, block)
    out_weight = out_weight.reshape(local_blocks, terms * block, block)

    def exchange(value):
        got = {bit: swapped(value, "feat", bit) for bit in far_first}
        return [got[bit] for bit in range(device_bits)]

    partners = []
    for s in range(seqs):
        partners.append(exchange(stage(tokens, s, partners[s - 2] if s >= 2 else [])))

    gains = jnp.stack([norm_gain] + exchange(norm_gain))
    x_full = tokens.astype(jnp.float32)
    row_squares = lax.psum(jnp.sum(x_full * x_full, axis=-1), "feat")
    scale = lax.rsqrt(row_squares / D + 1e-05)[..., None]
    index = lax.axis_index("ctx") * rows + jnp.arange(rows, dtype=jnp.int32)
    reach = jnp.minimum(jnp.minimum(positions, index), WINDOW - 1)[..., None]

    result = None
    blocks = []
    for s in range(seqs):
        q, kv, tail = project(
            section_bits, tokens, s, partners[s], scale, gains, qkv_weight
        )
        rim = passed_along(tail, "ctx", 1)
        attended = attend(q, kv, rim, reach, s)
        blocks.append([attended] + exchange(attended))
    for s in range(seqs):
        result = finish(section_bits, blocks[s], tokens, s, out_weight, result)
    return result


def solution(mesh):
    in_specs = (
        P(None, "ctx", "feat"),
        P("feat"),
        P(None, "feat", None, None, None),
        P("feat", None, None, None),
        P(),
        P(None, "ctx"),
    )
    out_specs = P(None, "ctx", "feat")
    return jax.shard_map(
        per_device, mesh=mesh, in_specs=in_specs, out_specs=out_specs, check_vma=False
    )
```

```python
import functools

import jax
import jax.numpy as jnp
from jax import lax
from jax.experimental import pallas as pl
from jax.experimental.pallas import tpu as pltpu
from jax.sharding import PartitionSpec as P

D = 8192
WINDOW = 128
HEAD = 128
VMEM_LIMIT = 48 * 2**20


def swapped(value, axis, bit):
    mask = 2**bit
    pairs = [(source, source ^ mask) for source in range(lax.axis_size(axis))]
    return lax.ppermute(value, axis, pairs)


def passed_along(shard, axis, by):
    devices = lax.axis_size(axis)
    pairs = [(i, i + by) for i in range(devices) if 0 <= i + by < devices]
    return lax.ppermute(shard, axis, pairs)


def params():
    return pltpu.CompilerParams(
        dimension_semantics=("arbitrary",), vmem_limit_bytes=VMEM_LIMIT
    )


def partner_slots(bits_ref, i, local_blocks, sections):
    local_bits = local_blocks.bit_length() - 1
    slots = [i]
    for s in range(sections):
        bit = bits_ref[s]
        near = lax.bitwise_xor(i, lax.shift_left(jnp.int32(1), bit))
        far = (1 + bit - local_bits) * local_blocks + i
        slots.append(jnp.where(bit < local_bits, near, far))
    return slots


def stage_kernel(x_ref, *rest):
    rest[-1][...] = x_ref[0]


def stage(tokens, s, after):
    seqs, rows, width = tokens.shape
    return pl.pallas_call(
        stage_kernel,
        grid=(1,),
        in_specs=[pl.BlockSpec((1, rows, width), lambda i: (s, 0, 0))]
        + [pl.BlockSpec(memory_space=pl.ANY)] * len(after),
        out_specs=pl.BlockSpec((rows, width), lambda i: (0, 0)),
        out_shape=jax.ShapeDtypeStruct((rows, width), tokens.dtype),
        compiler_params=params(),
        cost_estimate=pl.CostEstimate(
            flops=0, bytes_accessed=4 * rows * width, transcendentals=0
        ),
        name="stage",
    )(tokens, *after)


def qkv_kernel(parts, local_blocks, sections, bits_ref, *refs):
    x_refs = refs[:parts]
    scale_ref, gain_ref, w_ref = refs[parts : parts + 3]
    q_ref, kv_ref, tail_ref, normed = refs[-4:]
    i = pl.program_id(0)
    block = w_ref.shape[-1]

    @pl.when(i == 0)
    def _():
        scale = scale_ref[0]
        for part in range(parts):
            for b in range(local_blocks):
                lanes = slice(b * block, (b + 1) * block)
                x = x_refs[part][0, :, lanes] if part == 0 else x_refs[part][:, lanes]
                x = x.astype(jnp.float32) * scale * gain_ref[part : part + 1, lanes]
                normed[part * local_blocks + b] = x.astype(jnp.bfloat16)

    slots = partner_slots(bits_ref, i, local_blocks, sections)
    lhs = jnp.concatenate([normed[slot] for slot in slots], axis=1)
    rows = lhs.shape[0]
    for m in range(3):
        out = jnp.dot(lhs, w_ref[m, 0], preferred_element_type=jnp.float32)
        out = out.astype(jnp.bfloat16)
        if m == 0:
            q_ref[...] = out
        else:
            kv_ref[m - 1] = out
            tail_ref[m - 1] = out[rows - WINDOW :]


def project(section_bits, tokens, s, partners, scale, gains, weight, after):
    seqs, rows, width = tokens.shape
    _, local_blocks, depth, block = weight.shape
    sections = section_bits.shape[0]
    parts = 1 + len(partners)
    whole = lambda i, bits: (0, 0)
    bf16 = jnp.bfloat16
    return pl.pallas_call(
        functools.partial(qkv_kernel, parts, local_blocks, sections),
        grid_spec=pltpu.PrefetchScalarGridSpec(
            num_scalar_prefetch=1,
            grid=(local_blocks,),
            in_specs=[pl.BlockSpec((1, rows, width), lambda i, bits: (s, 0, 0))]
            + [pl.BlockSpec((rows, width), whole)] * len(partners)
            + [
                pl.BlockSpec((1, rows, 1), lambda i, bits: (s, 0, 0)),
                pl.BlockSpec((parts, width), whole),
                pl.BlockSpec((3, 1, depth, block), lambda i, bits: (0, i, 0, 0)),
            ]
            + [pl.BlockSpec(memory_space=pl.ANY)] * len(after),
            out_specs=[
                pl.BlockSpec((rows, block), lambda i, bits: (0, i)),
                pl.BlockSpec((2, rows, block), lambda i, bits: (0, 0, i)),
                pl.BlockSpec((2, WINDOW, block), lambda i, bits: (0, 0, i)),
            ],
            scratch_shapes=[pltpu.VMEM((parts * local_blocks, rows, block), bf16)],
        ),
        out_shape=[
            jax.ShapeDtypeStruct((rows, width), bf16),
            jax.ShapeDtypeStruct((2, rows, width), bf16),
            jax.ShapeDtypeStruct((2, WINDOW, width), bf16),
        ],
        compiler_params=params(),
        cost_estimate=pl.CostEstimate(
            flops=6 * rows * depth * width,
            bytes_accessed=2 * weight.size + 2 * rows * width * (parts + 4),
            transcendentals=0,
        ),
        name="project",
    )(section_bits, tokens, *partners, scale, gains, weight, *after)


def attend_kernel(q_ref, kv_ref, rim_ref, reach_ref, *rest):
    out_ref = rest[-1]
    rows, width = q_ref.shape
    for c in range(rows // WINDOW):
        here = slice(c * WINDOW, (c + 1) * WINDOW)
        row = lax.broadcasted_iota(jnp.int32, (WINDOW, 2 * WINDOW), 0)
        col = lax.broadcasted_iota(jnp.int32, (WINDOW, 2 * WINDOW), 1)
        dist = row + WINDOW - col
        valid = (dist >= 0) & (dist <= reach_ref[0, here])
        for h in range(width // HEAD):
            lanes = slice(h * HEAD, (h + 1) * HEAD)
            near = []
            for m in range(2):
                if c == 0:
                    before = rim_ref[m, :, lanes]
                else:
                    before = kv_ref[m, (c - 1) * WINDOW : c * WINDOW, lanes]
                near.append(jnp.concatenate([before, kv_ref[m, here, lanes]], axis=0))
            scores = lax.dot_general(
                q_ref[here, lanes],
                near[0],
                (((1,), (1,)), ((), ())),
                preferred_element_type=jnp.float32,
            )
            masked = jnp.where(valid, scores * HEAD ** (-0.5), -1e30)
            top = jnp.max(masked, axis=-1, keepdims=True)
            expo = jnp.exp(masked - top)
            total = jnp.sum(expo, axis=-1, keepdims=True)
            weights = (expo * (1.0 / total)).astype(jnp.bfloat16)
            mixed = jnp.dot(weights, near[1], preferred_element_type=jnp.float32)
            out_ref[here, lanes] = mixed.astype(jnp.bfloat16)


def attend(q, kv, rim, reach, s, after):
    rows, width = q.shape
    step = min(width, 4 * HEAD)
    return pl.pallas_call(
        attend_kernel,
        grid=(width // step,),
        in_specs=[
            pl.BlockSpec((rows, step), lambda i: (0, i)),
            pl.BlockSpec((2, rows, step), lambda i: (0, 0, i)),
            pl.BlockSpec((2, WINDOW, step), lambda i: (0, 0, i)),
            pl.BlockSpec((1, rows, 1), lambda i: (s, 0, 0)),
        ]
        + [pl.BlockSpec(memory_space=pl.ANY)] * len(after),
        out_specs=pl.BlockSpec((rows, step), lambda i: (0, i)),
        out_shape=jax.ShapeDtypeStruct((rows, width), jnp.bfloat16),
        compiler_params=params(),
        cost_estimate=pl.CostEstimate(
            flops=8 * rows * WINDOW * width,
            bytes_accessed=2 * rows * width * 5,
            transcendentals=2 * rows * WINDOW * (width // HEAD),
        ),
        name="attend",
    )(q, kv, rim, reach, *after)


def out_kernel(parts, local_blocks, sections, bits_ref, *refs):
    a_refs = refs[:parts]
    x_ref, w_ref = refs[parts : parts + 2]
    out_ref, gathered = refs[-2:]
    i = pl.program_id(0)
    block = w_ref.shape[-1]

    @pl.when(i == 0)
    def _():
        for part in range(parts):
            for b in range(local_blocks):
                lanes = slice(b * block, (b + 1) * block)
                gathered[part * local_blocks + b] = a_refs[part][:, lanes]

    slots = partner_slots(bits_ref, i, local_blocks, sections)
    lhs = jnp.concatenate([gathered[slot] for slot in slots], axis=1)
    out = jnp.dot(lhs, w_ref[0], preferred_element_type=jnp.float32)
    out_ref[0] = x_ref[0].astype(jnp.float32) + out


def finish(section_bits, blocks, tokens, s, weight, result, after):
    seqs, rows, width = tokens.shape
    local_blocks, depth, block = weight.shape
    sections = section_bits.shape[0]
    parts = len(blocks)
    one = lambda i, bits: (s, 0, i)
    earlier = ([] if result is None else [result]) + after
    return pl.pallas_call(
        functools.partial(out_kernel, parts, local_blocks, sections),
        grid_spec=pltpu.PrefetchScalarGridSpec(
            num_scalar_prefetch=1,
            grid=(local_blocks,),
            in_specs=[pl.BlockSpec((rows, width), lambda i, bits: (0, 0))] * parts
            + [
                pl.BlockSpec((1, rows, block), one),
                pl.BlockSpec((1, depth, block), lambda i, bits: (i, 0, 0)),
            ]
            + [pl.BlockSpec(memory_space=pl.ANY)] * len(earlier),
            out_specs=pl.BlockSpec((1, rows, block), one),
            scratch_shapes=[
                pltpu.VMEM((parts * local_blocks, rows, block), jnp.bfloat16)
            ],
        ),
        out_shape=jax.ShapeDtypeStruct(tokens.shape, jnp.float32),
        input_output_aliases={} if result is None else {3 + parts: 0},
        compiler_params=params(),
        cost_estimate=pl.CostEstimate(
            flops=2 * rows * depth * width,
            bytes_accessed=2 * weight.size + rows * width * (2 * parts + 6),
            transcendentals=0,
        ),
        name="finish",
    )(section_bits, *blocks, tokens, weight, *earlier)


def per_device(tokens, norm_gain, qkv_weight, out_weight, section_bits, positions):
    seqs, rows, width = tokens.shape
    _, local_blocks, terms, block, _ = qkv_weight.shape
    device_bits = lax.axis_size("feat").bit_length() - 1
    far_first = list(range(device_bits))[::-1]
    qkv_weight = qkv_weight.reshape(3, local_blocks, terms * block, block)
    out_weight = out_weight.reshape(local_blocks, terms * block, block)

    def exchange(value):
        got = {bit: swapped(value, "feat", bit) for bit in far_first}
        return [got[bit] for bit in range(device_bits)]

    x_full = tokens.astype(jnp.float32)
    row_squares = jnp.sum(x_full * x_full, axis=-1).reshape(-1)
    note = jnp.concatenate([row_squares, norm_gain])
    notes = {}
    for mask in range(1, lax.axis_size("feat")):
        pairs = [(a, a ^ mask) for a in range(lax.axis_size("feat"))]
        notes[mask] = lax.ppermute(note, "feat", pairs)
    total = row_squares + sum(value[: seqs * rows] for value in notes.values())
    scale = lax.rsqrt(total / D + 1e-05).reshape(seqs, rows, 1)
    gains = jnp.stack(
        [norm_gain] + [notes[1 << bit][seqs * rows :] for bit in range(device_bits)]
    )
    index = lax.axis_index("ctx") * rows + jnp.arange(rows, dtype=jnp.int32)
    reach = jnp.minimum(jnp.minimum(positions, index), WINDOW - 1)[..., None]

    ahead = 2
    staged, partners, blocks, pending = {}, {}, {}, {}
    result = None
    last = None
    for t in range(seqs + 3 * ahead):
        if t < seqs:
            after = partners[t - ahead] if t >= ahead else list(notes.values())
            staged[t] = stage(tokens, t, after)
            partners[t] = exchange(staged[t])
            last = staged[t]
        s = t - 2 * ahead
        if 0 <= s < seqs:
            q, kv, rim = pending.pop(s)
            arrived = partners[t - ahead] if t - ahead < seqs else blocks[s - ahead]
            last = attend(q, kv, rim, reach, s, arrived)
            blocks[s] = [last] + exchange(last)
        s = t - ahead
        if 0 <= s < seqs:
            q, kv, tail = project(
                section_bits, tokens, s, partners[s], scale, gains, qkv_weight, [last]
            )
            pending[s] = (q, kv, passed_along(tail, "ctx", 1))
        s = t - 3 * ahead
        if 0 <= s < seqs:
            result = finish(
                section_bits, blocks[s], tokens, s, out_weight, result, [last]
            )
    return result


def solution(mesh):
    in_specs = (
        P(None, "ctx", "feat"),
        P("feat"),
        P(None, "feat", None, None, None),
        P("feat", None, None, None),
        P(),
        P(None, "ctx"),
    )
    out_specs = P(None, "ctx", "feat")
    return jax.shard_map(
        per_device, mesh=mesh, in_specs=in_specs, out_specs=out_specs, check_vma=False
    )
```

```python
import functools

import jax
import jax.numpy as jnp
from jax import lax
from jax.experimental import pallas as pl
from jax.experimental.pallas import tpu as pltpu
from jax.sharding import PartitionSpec as P

D = 8192
WINDOW = 128
HEAD = 128
VMEM_LIMIT = 48 * 2**20


def swapped(value, axis, bit):
    mask = 2**bit
    pairs = [(source, source ^ mask) for source in range(lax.axis_size(axis))]
    return lax.ppermute(value, axis, pairs)


def passed_along(shard, axis, by):
    devices = lax.axis_size(axis)
    pairs = [(i, i + by) for i in range(devices) if 0 <= i + by < devices]
    return lax.ppermute(shard, axis, pairs)


def params():
    return pltpu.CompilerParams(
        dimension_semantics=("arbitrary",), vmem_limit_bytes=VMEM_LIMIT
    )


def partner_slots(bits_ref, i, local_blocks, sections):
    local_bits = local_blocks.bit_length() - 1
    slots = [i]
    for s in range(sections):
        bit = bits_ref[s]
        near = lax.bitwise_xor(i, lax.shift_left(jnp.int32(1), bit))
        far = (1 + bit - local_bits) * local_blocks + i
        slots.append(jnp.where(bit < local_bits, near, far))
    return slots


def stage_kernel(x_ref, *rest):
    rest[-1][...] = x_ref[0]


def stage(tokens, s, after):
    seqs, rows, width = tokens.shape
    return pl.pallas_call(
        stage_kernel,
        grid=(1,),
        in_specs=[pl.BlockSpec((1, rows, width), lambda i: (s, 0, 0))]
        + [pl.BlockSpec(memory_space=pl.ANY)] * len(after),
        out_specs=pl.BlockSpec((rows, width), lambda i: (0, 0)),
        out_shape=jax.ShapeDtypeStruct((rows, width), tokens.dtype),
        compiler_params=params(),
        cost_estimate=pl.CostEstimate(
            flops=0, bytes_accessed=4 * rows * width, transcendentals=0
        ),
        name="stage",
    )(tokens, *after)


def qkv_kernel(parts, local_blocks, sections, bits_ref, *refs):
    x_refs = refs[:parts]
    scale_ref, gain_ref, w_ref = refs[parts : parts + 3]
    q_ref, kv_ref, tail_ref, normed = refs[-4:]
    i = pl.program_id(0)
    block = w_ref.shape[-1]

    @pl.when(i == 0)
    def _():
        scale = scale_ref[0]
        for part in range(parts):
            for b in range(local_blocks):
                lanes = slice(b * block, (b + 1) * block)
                x = x_refs[part][0, :, lanes] if part == 0 else x_refs[part][:, lanes]
                x = x.astype(jnp.float32) * scale * gain_ref[part : part + 1, lanes]
                normed[part * local_blocks + b] = x.astype(jnp.bfloat16)

    slots = partner_slots(bits_ref, i, local_blocks, sections)
    lhs = jnp.concatenate([normed[slot] for slot in slots], axis=1)
    rows = lhs.shape[0]
    for m in range(3):
        out = jnp.dot(lhs, w_ref[m, 0], preferred_element_type=jnp.float32)
        out = out.astype(jnp.bfloat16)
        if m == 0:
            q_ref[...] = out
        else:
            kv_ref[m - 1] = out
            tail_ref[m - 1] = out[rows - WINDOW :]


def project(section_bits, tokens, s, partners, scale, gains, weight, after):
    seqs, rows, width = tokens.shape
    _, local_blocks, depth, block = weight.shape
    sections = section_bits.shape[0]
    parts = 1 + len(partners)
    whole = lambda i, bits: (0, 0)
    bf16 = jnp.bfloat16
    return pl.pallas_call(
        functools.partial(qkv_kernel, parts, local_blocks, sections),
        grid_spec=pltpu.PrefetchScalarGridSpec(
            num_scalar_prefetch=1,
            grid=(local_blocks,),
            in_specs=[pl.BlockSpec((1, rows, width), lambda i, bits: (s, 0, 0))]
            + [pl.BlockSpec((rows, width), whole)] * len(partners)
            + [
                pl.BlockSpec((1, rows, 1), lambda i, bits: (s, 0, 0)),
                pl.BlockSpec((parts, width), whole),
                pl.BlockSpec((3, 1, depth, block), lambda i, bits: (0, i, 0, 0)),
            ]
            + [pl.BlockSpec(memory_space=pl.ANY)] * len(after),
            out_specs=[
                pl.BlockSpec((rows, block), lambda i, bits: (0, i)),
                pl.BlockSpec((2, rows, block), lambda i, bits: (0, 0, i)),
                pl.BlockSpec((2, WINDOW, block), lambda i, bits: (0, 0, i)),
            ],
            scratch_shapes=[pltpu.VMEM((parts * local_blocks, rows, block), bf16)],
        ),
        out_shape=[
            jax.ShapeDtypeStruct((rows, width), bf16),
            jax.ShapeDtypeStruct((2, rows, width), bf16),
            jax.ShapeDtypeStruct((2, WINDOW, width), bf16),
        ],
        compiler_params=params(),
        cost_estimate=pl.CostEstimate(
            flops=6 * rows * depth * width,
            bytes_accessed=2 * weight.size + 2 * rows * width * (parts + 4),
            transcendentals=0,
        ),
        name="project",
    )(section_bits, tokens, *partners, scale, gains, weight, *after)


def attend_kernel(q_ref, kv_ref, rim_ref, reach_ref, *rest):
    out_ref = rest[-1]
    rows, width = q_ref.shape
    for c in range(rows // WINDOW):
        here = slice(c * WINDOW, (c + 1) * WINDOW)
        row = lax.broadcasted_iota(jnp.int32, (WINDOW, 2 * WINDOW), 0)
        col = lax.broadcasted_iota(jnp.int32, (WINDOW, 2 * WINDOW), 1)
        dist = row + WINDOW - col
        valid = (dist >= 0) & (dist <= reach_ref[0, here])
        for h in range(width // HEAD):
            lanes = slice(h * HEAD, (h + 1) * HEAD)
            near = []
            for m in range(2):
                if c == 0:
                    before = rim_ref[m, :, lanes]
                else:
                    before = kv_ref[m, (c - 1) * WINDOW : c * WINDOW, lanes]
                near.append(jnp.concatenate([before, kv_ref[m, here, lanes]], axis=0))
            scores = lax.dot_general(
                q_ref[here, lanes],
                near[0],
                (((1,), (1,)), ((), ())),
                preferred_element_type=jnp.float32,
            )
            masked = jnp.where(valid, scores * HEAD ** (-0.5), -1e30)
            top = jnp.max(masked, axis=-1, keepdims=True)
            expo = jnp.exp(masked - top)
            total = jnp.sum(expo, axis=-1, keepdims=True)
            weights = (expo * (1.0 / total)).astype(jnp.bfloat16)
            mixed = jnp.dot(weights, near[1], preferred_element_type=jnp.float32)
            out_ref[here, lanes] = mixed.astype(jnp.bfloat16)


def attend(q, kv, rim, reach, s, after):
    rows, width = q.shape
    step = min(width, 4 * HEAD)
    return pl.pallas_call(
        attend_kernel,
        grid=(width // step,),
        in_specs=[
            pl.BlockSpec((rows, step), lambda i: (0, i)),
            pl.BlockSpec((2, rows, step), lambda i: (0, 0, i)),
            pl.BlockSpec((2, WINDOW, step), lambda i: (0, 0, i)),
            pl.BlockSpec((1, rows, 1), lambda i: (s, 0, 0)),
        ]
        + [pl.BlockSpec(memory_space=pl.ANY)] * len(after),
        out_specs=pl.BlockSpec((rows, step), lambda i: (0, i)),
        out_shape=jax.ShapeDtypeStruct((rows, width), jnp.bfloat16),
        compiler_params=params(),
        cost_estimate=pl.CostEstimate(
            flops=8 * rows * WINDOW * width,
            bytes_accessed=2 * rows * width * 5,
            transcendentals=2 * rows * WINDOW * (width // HEAD),
        ),
        name="attend",
    )(q, kv, rim, reach, *after)


def out_kernel(parts, local_blocks, sections, bits_ref, *refs):
    a_refs = refs[:parts]
    x_ref, w_ref = refs[parts : parts + 2]
    out_ref, gathered = refs[-2:]
    i = pl.program_id(0)
    block = w_ref.shape[-1]

    @pl.when(i == 0)
    def _():
        for part in range(parts):
            for b in range(local_blocks):
                lanes = slice(b * block, (b + 1) * block)
                gathered[part * local_blocks + b] = a_refs[part][:, lanes]

    slots = partner_slots(bits_ref, i, local_blocks, sections)
    lhs = jnp.concatenate([gathered[slot] for slot in slots], axis=1)
    out = jnp.dot(lhs, w_ref[0], preferred_element_type=jnp.float32)
    out_ref[0] = x_ref[0].astype(jnp.float32) + out


def finish(section_bits, blocks, tokens, s, weight, result, after):
    seqs, rows, width = tokens.shape
    local_blocks, depth, block = weight.shape
    sections = section_bits.shape[0]
    parts = len(blocks)
    one = lambda i, bits: (s, 0, i)
    earlier = ([] if result is None else [result]) + after
    return pl.pallas_call(
        functools.partial(out_kernel, parts, local_blocks, sections),
        grid_spec=pltpu.PrefetchScalarGridSpec(
            num_scalar_prefetch=1,
            grid=(local_blocks,),
            in_specs=[pl.BlockSpec((rows, width), lambda i, bits: (0, 0))] * parts
            + [
                pl.BlockSpec((1, rows, block), one),
                pl.BlockSpec((1, depth, block), lambda i, bits: (i, 0, 0)),
            ]
            + [pl.BlockSpec(memory_space=pl.ANY)] * len(earlier),
            out_specs=pl.BlockSpec((1, rows, block), one),
            scratch_shapes=[
                pltpu.VMEM((parts * local_blocks, rows, block), jnp.bfloat16)
            ],
        ),
        out_shape=jax.ShapeDtypeStruct(tokens.shape, jnp.float32),
        input_output_aliases={} if result is None else {3 + parts: 0},
        compiler_params=params(),
        cost_estimate=pl.CostEstimate(
            flops=2 * rows * depth * width,
            bytes_accessed=2 * weight.size + rows * width * (2 * parts + 6),
            transcendentals=0,
        ),
        name="finish",
    )(section_bits, *blocks, tokens, weight, *earlier)


def near_kernel(local_blocks, own_sections, sec_ref, *refs):
    a_ref, x_ref, w_ref = refs[:3]
    out_ref, gathered = refs[-2:]
    i = pl.program_id(0)
    block = w_ref.shape[-1]

    @pl.when(i == 0)
    def _():
        for b in range(local_blocks):
            gathered[b] = a_ref[:, b * block : (b + 1) * block]

    out = x_ref[0].astype(jnp.float32)
    out = out + jnp.dot(
        gathered[i], w_ref[0, :block], preferred_element_type=jnp.float32
    )
    for bit in range(own_sections):
        first = pl.multiple_of(sec_ref[bit] * block, block)
        out = out + jnp.dot(
            gathered[lax.bitwise_xor(i, jnp.int32(1 << bit))],
            w_ref[0, pl.ds(first, block)],
            preferred_element_type=jnp.float32,
        )
    out_ref[0] = out


def finish_near(sections_of, attended, tokens, s, weight, result, after):
    seqs, rows, width = tokens.shape
    local_blocks, depth, block = weight.shape
    one = lambda i, sec: (s, 0, i)
    earlier = ([] if result is None else [result]) + after
    return pl.pallas_call(
        functools.partial(near_kernel, local_blocks, local_blocks.bit_length() - 1),
        grid_spec=pltpu.PrefetchScalarGridSpec(
            num_scalar_prefetch=1,
            grid=(local_blocks,),
            in_specs=[
                pl.BlockSpec((rows, width), lambda i, sec: (0, 0)),
                pl.BlockSpec((1, rows, block), one),
                pl.BlockSpec((1, depth, block), lambda i, sec: (i, 0, 0)),
            ]
            + [pl.BlockSpec(memory_space=pl.ANY)] * len(earlier),
            out_specs=pl.BlockSpec((1, rows, block), one),
            scratch_shapes=[pltpu.VMEM((local_blocks, rows, block), jnp.bfloat16)],
        ),
        out_shape=jax.ShapeDtypeStruct(tokens.shape, jnp.float32),
        input_output_aliases={} if result is None else {4: 0},
        compiler_params=params(),
        cost_estimate=pl.CostEstimate(
            flops=2 * rows * depth * width,
            bytes_accessed=2 * weight.size + 8 * rows * width,
            transcendentals=0,
        ),
        name="finish_near",
    )(sections_of, attended, tokens, weight, *earlier)


def far_kernel(parts, sec_ref, *refs):
    out = refs[2 * parts][0]
    for part in range(parts):
        out = out + jnp.dot(
            refs[part][...], refs[parts + part][0], preferred_element_type=jnp.float32
        )
    refs[-1][0] = out


def finish_far(sections_of, partners, s, weight, result):
    seqs, rows, width = result.shape
    local_blocks, depth, block = weight.shape
    local_bits = local_blocks.bit_length() - 1
    parts = len(partners)
    one = pl.BlockSpec((1, rows, block), lambda i, sec: (s, 0, i))
    weight_of = [
        pl.BlockSpec((1, block, block), lambda i, sec, at=local_bits + d: (i, sec[at], 0))
        for d in range(parts)
    ]
    return pl.pallas_call(
        functools.partial(far_kernel, parts),
        grid_spec=pltpu.PrefetchScalarGridSpec(
            num_scalar_prefetch=1,
            grid=(local_blocks,),
            in_specs=[pl.BlockSpec((rows, block), lambda i, sec: (0, i))] * parts
            + weight_of
            + [one],
            out_specs=one,
        ),
        out_shape=jax.ShapeDtypeStruct(result.shape, jnp.float32),
        input_output_aliases={1 + 2 * parts: 0},
        compiler_params=params(),
        cost_estimate=pl.CostEstimate(
            flops=2 * rows * parts * block * width,
            bytes_accessed=2 * parts * block * width + rows * width * (2 * parts + 8),
            transcendentals=0,
        ),
        name="finish_far",
    )(sections_of, *partners, *[weight] * parts, result)


def per_device(tokens, norm_gain, qkv_weight, out_weight, section_bits, positions):
    seqs, rows, width = tokens.shape
    _, local_blocks, terms, block, _ = qkv_weight.shape
    device_bits = lax.axis_size("feat").bit_length() - 1
    far_first = list(range(device_bits))[::-1]
    qkv_weight = qkv_weight.reshape(3, local_blocks, terms * block, block)
    out_weight = out_weight.reshape(local_blocks, terms * block, block)

    def exchange(value):
        got = {bit: swapped(value, "feat", bit) for bit in far_first}
        return [got[bit] for bit in range(device_bits)]

    x_full = tokens.astype(jnp.float32)
    row_squares = jnp.sum(x_full * x_full, axis=-1).reshape(-1)
    note = jnp.concatenate([row_squares, norm_gain])
    notes = {}
    for mask in range(1, lax.axis_size("feat")):
        pairs = [(a, a ^ mask) for a in range(lax.axis_size("feat"))]
        notes[mask] = lax.ppermute(note, "feat", pairs)
    total = row_squares + sum(value[: seqs * rows] for value in notes.values())
    scale = lax.rsqrt(total / D + 1e-05).reshape(seqs, rows, 1)
    gains = jnp.stack(
        [norm_gain] + [notes[1 << bit][seqs * rows :] for bit in range(device_bits)]
    )
    index = lax.axis_index("ctx") * rows + jnp.arange(rows, dtype=jnp.int32)
    reach = jnp.minimum(jnp.minimum(positions, index), WINDOW - 1)[..., None]

    bit_ids = jnp.arange(section_bits.shape[0], dtype=jnp.int32)
    hits = section_bits[None, :] == bit_ids[:, None]
    sections_of = 1 + jnp.sum(jnp.where(hits, bit_ids[None, :], 0), axis=1)
    sections_of = sections_of.astype(jnp.int32)

    ahead = 2
    staged, partners, blocks, pending = {}, {}, {}, {}
    result = None
    last = None
    for t in range(seqs + 3 * ahead):
        if t < seqs:
            after = partners[t - ahead] if t >= ahead else [note]
            if t == 1:
                after = list(notes.values())
            staged[t] = stage(tokens, t, after)
            partners[t] = exchange(staged[t])
            last = staged[t]
        s = t - 2 * ahead
        if 0 <= s < seqs:
            q, kv, rim = pending.pop(s)
            arrived = partners[t - ahead] if t - ahead < seqs else blocks[s - ahead]
            last = attend(q, kv, rim, reach, s, arrived)
            blocks[s] = [last] + exchange(last)
        s = t - ahead
        if 0 <= s < seqs:
            q, kv, tail = project(
                section_bits, tokens, s, partners[s], scale, gains, qkv_weight, [last]
            )
            pending[s] = (q, kv, passed_along(tail, "ctx", 1))
        s = t - 3 * ahead
        if 0 <= s < seqs:
            if s < seqs - 1:
                result = finish(
                    section_bits, blocks[s], tokens, s, out_weight, result, [last]
                )
            else:
                result = finish_near(
                    sections_of, blocks[s][0], tokens, s, out_weight, result, [last]
                )
                result = finish_far(sections_of, blocks[s][1:], s, out_weight, result)
    return result


def solution(mesh):
    in_specs = (
        P(None, "ctx", "feat"),
        P("feat"),
        P(None, "feat", None, None, None),
        P("feat", None, None, None),
        P(),
        P(None, "ctx"),
    )
    out_specs = P(None, "ctx", "feat")
    return jax.shard_map(
        per_device, mesh=mesh, in_specs=in_specs, out_specs=out_specs, check_vma=False
    )
```
